32 devices in a mesh: gx: 16 (over z, y, core), gy: 2 (over x).
Axes of the slice: x: 2, y: 2, z: 4, core: 2. Of those that a mesh axis runs over, the one named last changes fastest.
Arguments:
- conserved: float32 [5, 16, 128, 256], P(None, None, 'gx', 'gy'), may hold values from -2.5 to 9, as said below
- register: float32 [5, 16, 128, 256], P(None, None, 'gx', 'gy'), may hold values from -1 to 1, as said below
- ghost_planes: float32 [5, 16, 128, 256], P(None, None, 'gx', 'gy'), may hold values from -2.5 to 9, as said below
Outputs:
- advanced: float32 [5, 16, 128, 256], P(None, None, 'gx', 'gy')
- carried: float32 [5, 16, 128, 256], P(None, None, 'gx', 'gy')
The draws below stay inside these ranges and needn't reach their ends.
Inputs may be any that keep to these rules, and one draw needn't show every extreme that they name: `conserved`: every cell holds density in [0.6, 1.4], velocity components of magnitude at most 1.5 and T = 1.4 p / rho in [0.7, 1.4]; energy is E = p / 0.4 + 0.5 rho |u|^2. `ghost_planes`: every cell holds density in [0.6, 1.4], velocity components of magnitude at most 1.5 and T = 1.4 p / rho in [0.7, 1.4]; energy is E = p / 0.4 + 0.5 rho |u|^2. `register`: the density row lies in [-0.25, 0.25]; the momentum and energy rows lie in [-1, 1]. Density stays at 0.3 or more through both sections.
All inputs are finite; a program needn't handle non-finite values.
Results may differ from the reference program's by a relative error of at most 0.00002.
Values sent between devices are 32-bit elements; how exact they have to be, the bound alone decides.
A program may use at most 64 MiB of HBM per device.

```python
import math
import jax
import jax.numpy as jnp
from jax import lax

NZ = 16
GZ = 8
NX = 128
NY = 256


adiabatic_exponent = 1.4


def physical(key, planes):
    noise_seed_keys = jax.random.split(key, 4)
    lattice_shape_sizes = (planes, NX, NY)
    fluid_specific_weight = 0.6 * jnp.exp(jax.random.uniform(noise_seed_keys[0], lattice_shape_sizes, jnp.float32) * math.log(1.4 / 0.6))
    kelvin_scalar_field = jax.random.uniform(noise_seed_keys[2], lattice_shape_sizes, jnp.float32, 0.7, 1.4)
    fluid_speed_vector = jnp.clip(0.4 * jax.random.normal(noise_seed_keys[1], (3,) + lattice_shape_sizes, jnp.float32), -1.2, 1.2)
    static_stress_scalar = fluid_specific_weight * kelvin_scalar_field / adiabatic_exponent
    energy = static_stress_scalar / (adiabatic_exponent - 1.0) + 0.5 * fluid_specific_weight * (fluid_speed_vector[0] * fluid_speed_vector[0] + fluid_speed_vector[1] * fluid_speed_vector[1] + fluid_speed_vector[2] * fluid_speed_vector[2])
    return jnp.concatenate([fluid_specific_weight[None], fluid_specific_weight[None] * fluid_speed_vector, energy[None]], axis=0)


def draw_conserved(key, part):
    return physical(jax.random.fold_in(key, 11), NZ)


def draw_ghost_planes(key, part):
    return physical(jax.random.fold_in(key, 23), 2 * GZ)


def draw_register(key, part):
    noise_seed_keys = jax.random.split(jax.random.fold_in(key, 37), 2)
    lattice_shape_sizes = (NZ, NX, NY)
    density_row = jnp.clip(0.1 * jax.random.normal(noise_seed_keys[0], (1,) + lattice_shape_sizes, jnp.float32), -0.25, 0.25)
    other_rows = jnp.clip(0.3 * jax.random.normal(noise_seed_keys[1], (4,) + lattice_shape_sizes, jnp.float32), -1.0, 1.0)
    return jnp.concatenate([density_row, other_rows], axis=0)


def setup_inputs(seed: int = 0) -> dict:
    key_list = jax.random.split(jax.random.key(seed), 4)
    conserved = draw_conserved(jax.random.fold_in(key_list[3], 71), 0)
    register = draw_register(jax.random.fold_in(key_list[3], 71), 0)
    ghost_planes = draw_ghost_planes(jax.random.fold_in(key_list[3], 71), 0)
    return dict(conserved=conserved, register=register, ghost_planes=ghost_planes)


adiabatic_exponent = 1.4
viscosity = 0.15
conductivity = 0.15 / (0.4 * 0.7)
time_step = 0.2
section_a = (-0.41789047, -1.19215169)
section_b = (0.37921031, 0.82295503)
stencil = (0.8, -0.2, 4.0 / 105.0, -1.0 / 280.0)
slab_planes = 4


def derivative(field, along):
    extent = field.shape[along]
    result = None
    for offset, weight in enumerate(stencil, start=1):
        term = weight * (lax.slice_in_dim(field, 4 + offset, extent - 4 + offset, axis=along)
                         - lax.slice_in_dim(field, 4 - offset, extent - 4 - offset, axis=along))
        result = term if result is None else result + term
    return result


def roll_derivative(field, along):
    result = None
    for offset, weight in enumerate(stencil, start=1):
        term = weight * (jnp.roll(field, -offset, axis=along) - jnp.roll(field, offset, axis=along))
        result = term if result is None else result + term
    return result


def primitives(conserved):
    fluid_specific_weight = conserved[0]
    fluid_speed_vector = conserved[1:4] / fluid_specific_weight
    kinetic = 0.5 * fluid_specific_weight * (fluid_speed_vector[0] * fluid_speed_vector[0] + fluid_speed_vector[1] * fluid_speed_vector[1] + fluid_speed_vector[2] * fluid_speed_vector[2])
    static_stress_scalar = (adiabatic_exponent - 1.0) * (conserved[4] - kinetic)
    kelvin_scalar_field = adiabatic_exponent * static_stress_scalar / fluid_specific_weight
    return jnp.concatenate([fluid_speed_vector, kelvin_scalar_field[None], static_stress_scalar[None]], axis=0)


def euler_flux(conserved, primitive, direction):
    speed = primitive[direction]
    static_stress_scalar = primitive[4]
    entries = [conserved[1 + direction]]
    for index in range(3):
        entry = conserved[1 + index] * speed
        if index == direction:
            entry = entry + static_stress_scalar
        entries.append(entry)
    entries.append((conserved[4] + static_stress_scalar) * speed)
    return jnp.stack(entries, axis=0)


def viscous_flux(grads, primitive, direction):
    dilation = grads[0] + grads[4] + grads[8]
    stresses = []
    for index in range(3):
        stress = viscosity * (grads[3 * index + direction] + grads[3 * direction + index])
        if index == direction:
            stress = stress - (2.0 / 3.0) * viscosity * dilation
        stresses.append(stress)
    energy = (primitive[0] * stresses[0] + primitive[1] * stresses[1] + primitive[2] * stresses[2]
              + conductivity * grads[9 + direction])
    return jnp.stack(stresses + [energy], axis=0)


def net_flux(conserved, primitive, viscous, direction):
    inviscid = euler_flux(conserved, primitive, direction)
    return jnp.concatenate([inviscid[:1], inviscid[1:] - viscous], axis=0)


def slab_tendency(slab_cells):
    primitive = primitives(slab_cells)
    fields = primitive[:4]
    grad_x = roll_derivative(fields[:, 4:-4], 2)
    grad_y = roll_derivative(fields[:, 4:-4], 3)
    grad_z = derivative(fields, 1)
    grads = jnp.stack([grad_x, grad_y, grad_z], axis=1).reshape((12,) + grad_z.shape[1:])
    middle = grads[:, 4:-4]
    mid_prim = primitive[:, 8:-8]
    mid_cons = slab_cells[:, 8:-8]
    flux_x = net_flux(mid_cons, mid_prim, viscous_flux(middle, mid_prim, 0), 0)
    flux_y = net_flux(mid_cons, mid_prim, viscous_flux(middle, mid_prim, 1), 1)
    flux_z = net_flux(slab_cells[:, 4:-4], primitive[:, 4:-4], viscous_flux(grads, primitive[:, 4:-4], 2), 2)
    return -(roll_derivative(flux_x, 2) + roll_derivative(flux_y, 3) + derivative(flux_z, 1))


def reference(conserved, register, ghost_planes):
    current = conserved
    for step_index in range(2):
        extended = jnp.concatenate([ghost_planes[:, :GZ], current, ghost_planes[:, GZ:]], axis=1)
        firsts = jnp.arange(NZ // slab_planes, dtype=jnp.int32) * slab_planes

        def one_slab(first_plane):
            slab_cells = lax.dynamic_slice_in_dim(extended, first_plane, slab_planes + 16, axis=1)
            return slab_tendency(slab_cells)

        blocks = lax.map(one_slab, firsts)
        tendency = jnp.moveaxis(blocks, 0, 1).reshape((5, NZ, NX, NY))
        register = section_a[step_index] * register + time_step * tendency
        current = current + section_b[step_index] * register
    return current, register
```

```python
import functools

import jax
import jax.numpy as jnp
from jax import lax
from jax.experimental import pallas as pl
from jax.experimental.pallas import tpu as pltpu
from jax.sharding import PartitionSpec as P

MESH = pl.DeviceIdType.MESH

viscosity = 0.15
conductivity = 0.15 / (0.4 * 0.7)
time_step = 0.2
section_a = (-0.41789047, -1.19215169)
section_b = (0.37921031, 0.82295503)
stencil = (0.8, -0.2, 4.0 / 105.0, -1.0 / 280.0)
CH = 4


def kernel(
    nx,
    ny,
    chunks,
    cons_hbm,
    reg_hbm,
    ghost_hbm,
    adv_hbm,
    car_hbm,
    QE,
    PR,
    REG,
    FX,
    FY,
    FZ,
    GH,
    XS,
    XR,
    YS,
    YR,
    XSG,
    XRG,
    YSG,
    YRG,
    in_sem,
    out_sem,
    xs_sem,
    xr_sem,
    ys_sem,
    yr_sem,
    gs_sem,
    gr_sem,
):
    ix = lax.axis_index("gx")
    iy = lax.axis_index("gy")
    right = lax.rem(ix + 1, nx)
    left = lax.rem(ix + nx - 1, nx)
    up = lax.rem(iy + 1, ny)
    down = lax.rem(iy + ny - 1, ny)
    y_sides = (0,) if ny == 2 else (0, 1)

    planes = chunks * CH
    ghost = ghost_hbm.shape[1] // 2
    loads = [
        pltpu.make_async_copy(cons_hbm, QE.at[:, pl.ds(ghost, planes)], in_sem.at[0]),
        pltpu.make_async_copy(ghost_hbm.at[:, pl.ds(0, ghost)], QE.at[:, pl.ds(0, ghost)], in_sem.at[1]),
        pltpu.make_async_copy(
            ghost_hbm.at[:, pl.ds(ghost, ghost)], QE.at[:, pl.ds(ghost + planes, ghost)], in_sem.at[2]
        ),
        pltpu.make_async_copy(reg_hbm, REG, in_sem.at[3]),
    ]
    for load in loads:
        load.start()

    barrier = pltpu.get_barrier_semaphore()
    pl.semaphore_signal(barrier, inc=1, device_id={"gx": left}, device_id_type=MESH)
    pl.semaphore_signal(barrier, inc=1, device_id={"gx": right}, device_id_type=MESH)
    for side in y_sides:
        pl.semaphore_signal(barrier, inc=1, device_id={"gy": (up, down)[side]}, device_id_type=MESH)

    sub = lax.broadcasted_iota(jnp.int32, (8, 128), 0)
    lane = lax.broadcasted_iota(jnp.int32, (8, 128), 1)
    low = sub < 4
    lane_group = lax.shift_right_logical(lane, 3)
    lane_first = lax.bitwise_and(lane, 7) < 4

    def x_send(way, r, c, fields):
        return pltpu.make_async_remote_copy(
            src_ref=XS.at[way, r, c, pl.ds(0, fields)],
            dst_ref=XR.at[way, r, c, pl.ds(0, fields)],
            send_sem=xs_sem.at[way, r, c],
            recv_sem=xr_sem.at[way, r, c],
            device_id={"gx": (right, left)[way]},
            device_id_type=MESH,
        )

    def y_send(way, r, c, count):
        return pltpu.make_async_remote_copy(
            src_ref=YS.at[r, c, pl.ds(0, count)],
            dst_ref=YR.at[way, r, c, pl.ds(0, count)],
            send_sem=ys_sem.at[way, r, c],
            recv_sem=yr_sem.at[way, r, c],
            device_id={"gy": (up, down)[way]},
            device_id_type=MESH,
        )

    def xg_send(way):
        return pltpu.make_async_remote_copy(
            src_ref=XSG.at[way],
            dst_ref=XRG.at[way],
            send_sem=gs_sem.at[way],
            recv_sem=gr_sem.at[way],
            device_id={"gx": (right, left)[way]},
            device_id_type=MESH,
        )

    def yg_send(way):
        return pltpu.make_async_remote_copy(
            src_ref=YSG,
            dst_ref=YRG.at[way],
            send_sem=gs_sem.at[2 + way],
            recv_sem=gr_sem.at[2 + way],
            device_id={"gy": (up, down)[way]},
            device_id_type=MESH,
        )

    def exchange(r, c):
        fields, count = ((4, 1), (5, 2))[r % 2]
        return [x_send(way, r, c, fields) for way in (0, 1)] + [y_send(way, r, c, count) for way in y_sides]

    def ghost_exchange():
        return [xg_send(way) for way in (0, 1)] + [yg_send(way) for way in y_sides]

    def pack_high(first, second):
        return jnp.where(low, pltpu.roll(second, 4, 0), first)

    def pack_low(first, second):
        return jnp.where(low, first, pltpu.roll(second, 4, 0))

    def unpack_x(from_left, from_right):
        first = jnp.where(low, from_right, from_left)
        second = pltpu.roll(jnp.where(low, from_left, from_right), 4, 0)
        return first, second

    def pack_y(items):
        packed = None
        for j, item in enumerate(items):
            turned = pltpu.roll(item, (8 * j + 4) % 128, 1)
            packed = turned if packed is None else jnp.where(lane_group == j, turned, packed)
        return packed

    def merge_y(ref, *index):
        if ny == 2:
            return ref[(0,) + index]
        return jnp.where(lane_first, ref[(0,) + index], ref[(1,) + index])

    def unpack_y(merged, j):
        return pltpu.roll(merged, (128 - (8 * j + 4)) % 128, 1)

    def d_x(field, halo):
        total = None
        for s, weight in enumerate(stencil[:3], start=1):
            plus = pltpu.roll(jnp.where(sub < s, halo, field), 8 - s, 0)
            minus = pltpu.roll(jnp.where(sub >= 8 - s, halo, field), s, 0)
            term = weight * (plus - minus)
            total = term if total is None else total + term
        gap = halo - field
        return total + stencil[3] * pltpu.roll(jnp.where(low, gap, -gap), 4, 0)

    def d_y(field, halo):
        total = None
        for s, weight in enumerate(stencil, start=1):
            plus = pltpu.roll(jnp.where(lane < s, halo, field), 128 - s, 1)
            minus = pltpu.roll(jnp.where(lane >= 128 - s, halo, field), s, 1)
            term = weight * (plus - minus)
            total = term if total is None else total + term
        return total

    def d_z(ref, f, z):
        total = None
        for s, weight in enumerate(stencil, start=1):
            term = weight * (ref[f, z + s] - ref[f, z - s])
            total = term if total is None else total + term
        return total

    def primitives(q):
        inverse = 1.0 / q[0]
        speeds = [q[1] * inverse, q[2] * inverse, q[3] * inverse]
        kinetic = 0.5 * (q[1] * speeds[0] + q[2] * speeds[1] + q[3] * speeds[2])
        pressure = 0.4 * (q[4] - kinetic)
        return speeds + [1.4 * pressure * inverse, pressure]

    def store_primitives(q, z):
        values = primitives(q)
        for f in range(5):
            PR[f, z] = values[f]
        return values

    def send_state(r, c, values):
        for f in range(4):
            for k in range(CH // 2):
                XS[0, r, c, f, k] = pack_high(values[k][f], values[k + 2][f])
                XS[1, r, c, f, k] = pack_low(values[k][f], values[k + 2][f])
        YS[r, c, 0] = pack_y([values[k][f] for f in range(4) for k in range(CH)])
        for copy in exchange(r, c):
            copy.start()

    def start_chunk(c, carry):
        values = []
        for k in range(CH):
            z = ghost + c * CH + k
            values.append(store_primitives([QE[f, z] for f in range(5)], z))
        send_state(0, c, values)
        return carry

    def ghost_start():
        near = []
        for z in list(range(ghost)) + list(range(ghost + planes, 2 * ghost + planes)):
            values = store_primitives([QE[f, z] for f in range(5)], z)
            if ghost - 4 <= z < ghost + planes + 4:
                near.append(values)
        for f, field in enumerate((0, 2)):
            for k in range(4):
                XSG[0, f, k] = pack_high(near[k][field], near[k + 4][field])
                XSG[1, f, k] = pack_low(near[k][field], near[k + 4][field])
        YSG[...] = pack_y([near[k][field] for field in (1, 2) for k in range(8)])
        for copy in ghost_exchange():
            copy.start()

    def vertical(z, grads, q, u, p):
        m1, m2, m3, energy = q
        txz, tyz, tzz, heat = grads
        FZ[0, z - 4] = m3
        FZ[1, z - 4] = m1 * u[2] - txz
        FZ[2, z - 4] = m2 * u[2] - tyz
        FZ[3, z - 4] = m3 * u[2] + p - tzz
        FZ[4, z - 4] = (energy + p) * u[2] - (u[0] * txz + u[1] * tyz + u[2] * tzz + heat)

    def flux_chunk(r, c, carry):
        for copy in exchange(r, c):
            copy.wait_recv()
        halos = [[None] * CH for _ in range(4)]
        for f in range(4):
            for k in range(CH // 2):
                halos[f][k], halos[f][k + 2] = unpack_x(XR[0, r, c, f, k], XR[1, r, c, f, k])
        merged = merge_y(YR, r, c, 0)
        packs_x = []
        packs_y = []
        for k in range(CH):
            z = ghost + c * CH + k
            value = [PR[f, z] for f in range(4)]
            gx = [d_x(value[f], halos[f][k]) for f in range(4)]
            gy = [d_y(value[f], unpack_y(merged, CH * f + k)) for f in range(4)]
            gz = [d_z(PR, f, z) for f in range(4)]
            u = value[:3]
            p = PR[4, z]
            m1, m2, m3, energy = [QE[f, z] for f in range(1, 5)]
            dilation = (2.0 / 3.0 * viscosity) * (gx[0] + gy[1] + gz[2])
            txx = (2.0 * viscosity) * gx[0] - dilation
            tyy = (2.0 * viscosity) * gy[1] - dilation
            tzz = (2.0 * viscosity) * gz[2] - dilation
            txy = viscosity * (gx[1] + gy[0])
            txz = viscosity * (gx[2] + gz[0])
            tyz = viscosity * (gy[2] + gz[1])
            total = energy + p
            flux_x = [
                m1,
                m1 * u[0] + p - txx,
                m2 * u[0] - txy,
                m3 * u[0] - txz,
                total * u[0] - (u[0] * txx + u[1] * txy + u[2] * txz + conductivity * gx[3]),
            ]
            flux_y = [
                m2,
                m1 * u[1] - txy,
                m2 * u[1] + p - tyy,
                m3 * u[1] - tyz,
                total * u[1] - (u[0] * txy + u[1] * tyy + u[2] * tyz + conductivity * gy[3]),
            ]
            for f in range(5):
                FX[f, c * CH + k] = flux_x[f]
                FY[f, c * CH + k] = flux_y[f]
            packs_x.append(flux_x)
            packs_y.append(flux_y)
            vertical(z, (txz, tyz, tzz, conductivity * gz[3]), (m1, m2, m3, energy), u, p)
        r = r + 1
        for f in range(5):
            for k in range(CH // 2):
                XS[0, r, c, f, k] = pack_high(packs_x[k][f], packs_x[k + 2][f])
                XS[1, r, c, f, k] = pack_low(packs_x[k][f], packs_x[k + 2][f])
        YS[r, c, 0] = pack_y([packs_y[k][f] for f in range(4) for k in range(CH)])
        YS[r, c, 1] = pack_y([packs_y[k][4] for k in range(CH)])
        for copy in exchange(r, c):
            copy.start()
        return carry

    def ghost_gradients():
        for copy in ghost_exchange():
            copy.wait_recv()
        halos = [[None] * 8 for _ in range(2)]
        for f in range(2):
            for k in range(4):
                halos[f][k], halos[f][k + 4] = unpack_x(XRG[0, f, k], XRG[1, f, k])
        merged = merge_y(YRG)
        for k in range(8):
            z = ghost - 4 + k if k < 4 else ghost + planes + k - 4
            u = [PR[f, z] for f in range(3)]
            GH[0, k] = d_x(u[0], halos[0][k]) + d_y(u[1], unpack_y(merged, k))
            GH[1, k] = d_x(u[2], halos[1][k])
            GH[2, k] = d_y(u[2], unpack_y(merged, 8 + k))

    def ghost_flux(k, carry):
        z = ghost - 4 + k + (planes + 4 - 4) * (k // 4)
        gz = [d_z(PR, f, z) for f in range(4)]
        dilation = (2.0 / 3.0 * viscosity) * (GH[0, k] + gz[2])
        tzz = (2.0 * viscosity) * gz[2] - dilation
        txz = viscosity * (GH[1, k] + gz[0])
        tyz = viscosity * (GH[2, k] + gz[1])
        vertical(
            z,
            (txz, tyz, tzz, conductivity * gz[3]),
            [QE[f, z] for f in range(1, 5)],
            [PR[f, z] for f in range(3)],
            PR[4, z],
        )
        return carry

    def outputs(c):
        return [
            pltpu.make_async_copy(
                QE.at[:, pl.ds(ghost + c * CH, CH)], adv_hbm.at[:, pl.ds(c * CH, CH)], out_sem.at[0, c]
            ),
            pltpu.make_async_copy(REG.at[:, pl.ds(c * CH, CH)], car_hbm.at[:, pl.ds(c * CH, CH)], out_sem.at[1, c]),
        ]

    def update_chunk(section, c, carry):
        r = 2 * section + 1
        for copy in exchange(r, c):
            copy.wait_recv()
        halos = [[None] * CH for _ in range(5)]
        for f in range(5):
            for k in range(CH // 2):
                halos[f][k], halos[f][k + 2] = unpack_x(XR[0, r, c, f, k], XR[1, r, c, f, k])
        merged = [merge_y(YR, r, c, 0), merge_y(YR, r, c, 1)]
        values = []
        for k in range(CH):
            w = c * CH + k
            z = ghost + w
            q = []
            for f in range(5):
                slope = d_x(FX[f, w], halos[f][k])
                slope += d_y(FY[f, w], unpack_y(merged[f // 4], CH * (f % 4) + k))
                slope += d_z(FZ, f, w + 4)
                register = section_a[section] * REG[f, w] - time_step * slope
                REG[f, w] = register
                state = QE[f, z] + section_b[section] * register
                QE[f, z] = state
                q.append(state)
            if section == 0:
                values.append(store_primitives(q, z))
        if section == 0:
            send_state(2, c, values)
        else:
            for copy in outputs(c):
                copy.start()
        return carry

    loads[0].wait()
    pl.semaphore_wait(barrier, 2 + len(y_sides))
    lax.fori_loop(0, chunks, start_chunk, 0)
    loads[1].wait()
    loads[2].wait()
    ghost_start()
    for section in range(2):
        lax.fori_loop(0, chunks, functools.partial(flux_chunk, 2 * section), 0)
        if section == 0:
            ghost_gradients()
            loads[3].wait()
        lax.fori_loop(0, 8, ghost_flux, 0)
        lax.fori_loop(0, chunks, functools.partial(update_chunk, section), 0)

    for copy in ghost_exchange():
        copy.wait_send()

    def finish(c, carry):
        for r in range(4):
            for copy in exchange(r, c):
                copy.wait_send()
        for copy in outputs(c):
            copy.wait()
        return carry

    lax.fori_loop(0, chunks, finish, 0)


def solution(mesh):
    nx, ny = mesh.shape["gx"], mesh.shape["gy"]

    def body(conserved, register, ghost_planes):
        _, planes, rows, columns = conserved.shape
        assert (rows, columns) == (8, 128) and planes % CH == 0
        chunks = planes // CH
        extended = planes + ghost_planes.shape[1]
        tile = (rows, columns)

        def vmem(*shape):
            return pltpu.VMEM(shape + tile, jnp.float32)

        dma = pltpu.SemaphoreType.DMA
        return pl.pallas_call(
            functools.partial(kernel, nx, ny, chunks),
            out_shape=[jax.ShapeDtypeStruct(conserved.shape, jnp.float32)] * 2,
            in_specs=[pl.BlockSpec(memory_space=pl.ANY)] * 3,
            out_specs=[pl.BlockSpec(memory_space=pl.ANY)] * 2,
            scratch_shapes=[
                vmem(5, extended),
                vmem(5, extended),
                vmem(5, planes),
                vmem(5, planes),
                vmem(5, planes),
                vmem(5, planes + 8),
                vmem(3, 8),
                vmem(2, 4, chunks, 5, CH // 2),
                vmem(2, 4, chunks, 5, CH // 2),
                vmem(4, chunks, 2),
                vmem(2, 4, chunks, 2),
                vmem(2, 2, 4),
                vmem(2, 2, 4),
                vmem(),
                vmem(2),
                dma((4,)),
                dma((2, chunks)),
                dma((2, 4, chunks)),
                dma((2, 4, chunks)),
                dma((2, 4, chunks)),
                dma((2, 4, chunks)),
                dma((4,)),
                dma((4,)),
            ],
            compiler_params=pltpu.CompilerParams(
                collective_id=0, has_side_effects=True, vmem_limit_bytes=40 * 1024 * 1024
            ),
        )(conserved, register, ghost_planes)

    spec = P(None, None, "gx", "gy")
    return jax.shard_map(
        body, mesh=mesh, in_specs=(spec, spec, spec), out_specs=(spec, spec), check_vma=False
    )
```

```python
import functools

import jax
import jax.numpy as jnp
from jax import lax
from jax.experimental import pallas as pl
from jax.experimental.pallas import tpu as pltpu
from jax.sharding import PartitionSpec as P

MESH = pl.DeviceIdType.MESH

viscosity = 0.15
conductivity = 0.15 / (0.4 * 0.7)
time_step = 0.2
section_a = (-0.41789047, -1.19215169)
section_b = (0.37921031, 0.82295503)
stencil = (0.8, -0.2, 4.0 / 105.0, -1.0 / 280.0)
CH = 4
HALF = CH // 2
Y_STATE = (4 * CH + 15) // 16
Y_FLUX = (5 * CH + 15) // 16


def kernel(
    nx,
    ny,
    chunks,
    cons_hbm,
    reg_hbm,
    ghost_hbm,
    state_out,
    register_out,
    slope_out,
    QE,
    PR,
    REG,
    FX,
    FY,
    FZ,
    GH,
    DX,
    DY,
    DZ,
    SL,
    XS,
    XR,
    YS,
    YR,
    XSG,
    XRG,
    YSG,
    YRG,
    in_sem,
    xs_sem,
    xr_sem,
    ys_sem,
    yr_sem,
    gs_sem,
    gr_sem,
):
    ix = lax.axis_index("gx")
    iy = lax.axis_index("gy")
    right = lax.rem(ix + 1, nx)
    left = lax.rem(ix + nx - 1, nx)
    up = lax.rem(iy + 1, ny)
    down = lax.rem(iy + ny - 1, ny)
    y_sides = (0,) if ny == 2 else (0, 1)

    planes = chunks * CH
    ghost = ghost_hbm.shape[1] // 2
    loads = [
        pltpu.make_async_copy(cons_hbm, QE.at[:, pl.ds(ghost, planes)], in_sem.at[0]),
        pltpu.make_async_copy(ghost_hbm.at[:, pl.ds(0, ghost)], QE.at[:, pl.ds(0, ghost)], in_sem.at[1]),
        pltpu.make_async_copy(
            ghost_hbm.at[:, pl.ds(ghost, ghost)], QE.at[:, pl.ds(ghost + planes, ghost)], in_sem.at[2]
        ),
        pltpu.make_async_copy(reg_hbm, REG, in_sem.at[3]),
    ]
    for load in loads:
        load.start()

    barrier = pltpu.get_barrier_semaphore()
    pl.semaphore_signal(barrier, inc=1, device_id={"gx": left}, device_id_type=MESH)
    pl.semaphore_signal(barrier, inc=1, device_id={"gx": right}, device_id_type=MESH)
    for side in y_sides:
        pl.semaphore_signal(barrier, inc=1, device_id={"gy": (up, down)[side]}, device_id_type=MESH)

    sub = lax.broadcasted_iota(jnp.int32, (8, 128), 0)
    lane = lax.broadcasted_iota(jnp.int32, (8, 128), 1)
    low = sub < 4
    lane_group = lax.shift_right_logical(lane, 3)
    lane_first = lax.bitwise_and(lane, 7) < 4

    def x_send(way, r, c, fields):
        return pltpu.make_async_remote_copy(
            src_ref=XS.at[way, r, c, pl.ds(0, fields)],
            dst_ref=XR.at[way, r, c, pl.ds(0, fields)],
            send_sem=xs_sem.at[way, r, c],
            recv_sem=xr_sem.at[way, r, c],
            device_id={"gx": (right, left)[way]},
            device_id_type=MESH,
        )

    def y_send(way, r, c, count):
        return pltpu.make_async_remote_copy(
            src_ref=YS.at[r, c, pl.ds(0, count)],
            dst_ref=YR.at[way, r, c, pl.ds(0, count)],
            send_sem=ys_sem.at[way, r, c],
            recv_sem=yr_sem.at[way, r, c],
            device_id={"gy": (up, down)[way]},
            device_id_type=MESH,
        )

    def xg_send(way):
        return pltpu.make_async_remote_copy(
            src_ref=XSG.at[way],
            dst_ref=XRG.at[way],
            send_sem=gs_sem.at[way],
            recv_sem=gr_sem.at[way],
            device_id={"gx": (right, left)[way]},
            device_id_type=MESH,
        )

    def yg_send(way):
        return pltpu.make_async_remote_copy(
            src_ref=YSG,
            dst_ref=YRG.at[way],
            send_sem=gs_sem.at[2 + way],
            recv_sem=gr_sem.at[2 + way],
            device_id={"gy": (up, down)[way]},
            device_id_type=MESH,
        )

    def exchange(r, c):
        fields, count = ((4, Y_STATE), (5, Y_FLUX))[r % 2]
        return [x_send(way, r, c, fields) for way in (0, 1)] + [y_send(way, r, c, count) for way in y_sides]

    def ghost_exchange():
        return [xg_send(way) for way in (0, 1)] + [yg_send(way) for way in y_sides]

    def pack_high(first, second):
        return jnp.where(low, pltpu.roll(second, 4, 0), first)

    def pack_low(first, second):
        return jnp.where(low, first, pltpu.roll(second, 4, 0))

    def unpack_x(from_left, from_right):
        first = jnp.where(low, from_right, from_left)
        second = pltpu.roll(jnp.where(low, from_left, from_right), 4, 0)
        return first, second

    row = lax.bitwise_and(sub, 3)
    column = lax.bitwise_and(lane, 7)
    edge = jnp.logical_or(lane < 4, lane >= 124)
    low_weights = [jnp.where(row + d <= 3, -stencil[3 - d], 0.0) for d in range(4)]
    high_weights = [jnp.where(row >= d, stencil[3 - d], 0.0) for d in range(4)]

    def inner_x(field):
        a, b, c, _ = stencil
        after = pltpu.roll(field, 7, 0)
        before = pltpu.roll(field, 1, 0)
        middle = b * field
        return pltpu.roll(a * before + middle + c * after, 6, 0) - pltpu.roll(a * after + middle + c * before, 2, 0)

    def inner_y(field):
        a, b, c, d = stencil
        after = pltpu.roll(field, 127, 1)
        before = pltpu.roll(field, 1, 1)
        middle = c * field
        far = pltpu.roll(b * before + middle + d * after, 125, 1) - pltpu.roll(b * after + middle + d * before, 3, 1)
        return a * (after - before) + far

    def edge_x(r, c, f, k):
        gap_low = XR[0, r, c, f, k] - XS[0, r, c, f, k]
        gap_high = XR[1, r, c, f, k] - XS[1, r, c, f, k]
        at_low = low_weights[0] * gap_low
        at_high = high_weights[0] * gap_high
        for d in range(1, 4):
            at_low += low_weights[d] * pltpu.roll(gap_low, 8 - d, 0)
            at_high += high_weights[d] * pltpu.roll(gap_high, d, 0)
        return pltpu.roll(jnp.where(low, at_high, at_low), 4, 0), jnp.where(low, at_low, at_high)

    def edge_y(merged, own):
        gap = merged - own
        total = None
        for o, weight in enumerate(stencil, start=1):
            at_high = jnp.logical_and(column < 4, column + o >= 4)
            at_low = jnp.logical_and(column >= 4, column - o < 4)
            term = jnp.where(at_high, weight, 0.0) * pltpu.roll(gap, 128 - o, 1)
            term += jnp.where(at_low, -weight, 0.0) * pltpu.roll(gap, o, 1)
            total = term if total is None else total + term
        return total

    def place_y(packed, j):
        packed, j = packed[j // 16], j % 16
        return jnp.where(edge, pltpu.roll(packed, (128 - (8 * j + 4)) % 128, 1), 0.0)

    def pack_y(items):
        packed = None
        for j, item in enumerate(items):
            turned = pltpu.roll(item, (8 * j + 4) % 128, 1)
            packed = turned if packed is None else jnp.where(lane_group == j, turned, packed)
        return packed

    def send_y(r, c, items):
        for i in range(0, len(items), 16):
            YS[r, c, i // 16] = pack_y(items[i : i + 16])

    def merge_y(ref, *index):
        if ny == 2:
            return ref[(0,) + index]
        return jnp.where(lane_first, ref[(0,) + index], ref[(1,) + index])

    def unpack_y(merged, j):
        return pltpu.roll(merged, (128 - (8 * j + 4)) % 128, 1)

    def d_x(field, halo):
        total = None
        for s, weight in enumerate(stencil, start=1):
            plus = pltpu.roll(jnp.where(sub < s, halo, field), 8 - s, 0)
            minus = pltpu.roll(jnp.where(sub >= 8 - s, halo, field), s, 0)
            term = weight * (plus - minus)
            total = term if total is None else total + term
        return total

    def d_y(field, halo):
        total = None
        for s, weight in enumerate(stencil, start=1):
            plus = pltpu.roll(jnp.where(lane < s, halo, field), 128 - s, 1)
            minus = pltpu.roll(jnp.where(lane >= 128 - s, halo, field), s, 1)
            term = weight * (plus - minus)
            total = term if total is None else total + term
        return total

    def d_z(ref, f, z):
        total = None
        for s, weight in enumerate(stencil, start=1):
            term = weight * (ref[f, z + s] - ref[f, z - s])
            total = term if total is None else total + term
        return total

    def primitives(q):
        inverse = 1.0 / q[0]
        speeds = [q[1] * inverse, q[2] * inverse, q[3] * inverse]
        kinetic = 0.5 * (q[1] * speeds[0] + q[2] * speeds[1] + q[3] * speeds[2])
        pressure = 0.4 * (q[4] - kinetic)
        return speeds + [1.4 * pressure * inverse, pressure]

    def store_primitives(q, z):
        values = primitives(q)
        for f in range(5):
            PR[f, z] = values[f]
        return values

    def send_state(r, c, values):
        for f in range(4):
            for k in range(HALF):
                XS[0, r, c, f, k] = pack_high(values[k][f], values[k + HALF][f])
                XS[1, r, c, f, k] = pack_low(values[k][f], values[k + HALF][f])
        send_y(r, c, [values[k][f] for f in range(4) for k in range(CH)])
        for copy in exchange(r, c):
            copy.start()

    def start_chunk(c, carry):
        values = []
        for k in range(CH):
            z = ghost + c * CH + k
            values.append(store_primitives([QE[f, z] for f in range(5)], z))
        send_state(0, c, values)
        return carry

    def ghost_start():
        near = []
        for z in list(range(ghost)) + list(range(ghost + planes, 2 * ghost + planes)):
            values = store_primitives([QE[f, z] for f in range(5)], z)
            if ghost - 4 <= z < ghost + planes + 4:
                near.append(values)
        for f, field in enumerate((0, 2)):
            for k in range(4):
                XSG[0, f, k] = pack_high(near[k][field], near[k + 4][field])
                XSG[1, f, k] = pack_low(near[k][field], near[k + 4][field])
        YSG[...] = pack_y([near[k][field] for field in (1, 2) for k in range(8)])
        for copy in ghost_exchange():
            copy.start()

    def vertical(z, grads, q, u, p):
        m1, m2, m3, energy = q
        txz, tyz, tzz, heat = grads
        FZ[0, z - 4] = m3
        FZ[1, z - 4] = m1 * u[2] - txz
        FZ[2, z - 4] = m2 * u[2] - tyz
        FZ[3, z - 4] = m3 * u[2] + p - tzz
        FZ[4, z - 4] = (energy + p) * u[2] - (u[0] * txz + u[1] * tyz + u[2] * tzz + heat)

    def gradient_chunk(c, carry):
        for k in range(CH):
            w = c * CH + k
            for f in range(4):
                field = PR[f, ghost + w]
                DX[f, w] = inner_x(field)
                DY[f, w] = inner_y(field)
                DZ[f, w] = d_z(PR, f, ghost + w)
        return carry

    def flux_chunk(r, c, carry):
        for copy in exchange(r, c):
            copy.wait_recv()
        edges = [[None] * CH for _ in range(4)]
        for f in range(4):
            for k in range(HALF):
                edges[f][k], edges[f][k + HALF] = edge_x(r, c, f, k)
        packed = [edge_y(merge_y(YR, r, c, i), YS[r, c, i]) for i in range(Y_STATE)]
        packs_x = []
        packs_y = []
        for k in range(CH):
            z = ghost + c * CH + k
            value = [PR[f, z] for f in range(4)]
            w = c * CH + k
            gx = [DX[f, w] + edges[f][k] for f in range(4)]
            gy = [DY[f, w] + place_y(packed, CH * f + k) for f in range(4)]
            gz = [DZ[f, w] for f in range(4)]
            u = value[:3]
            p = PR[4, z]
            m1, m2, m3, energy = [QE[f, z] for f in range(1, 5)]
            dilation = (2.0 / 3.0 * viscosity) * (gx[0] + gy[1] + gz[2])
            txx = (2.0 * viscosity) * gx[0] - dilation
            tyy = (2.0 * viscosity) * gy[1] - dilation
            tzz = (2.0 * viscosity) * gz[2] - dilation
            txy = viscosity * (gx[1] + gy[0])
            txz = viscosity * (gx[2] + gz[0])
            tyz = viscosity * (gy[2] + gz[1])
            total = energy + p
            flux_x = [
                m1,
                m1 * u[0] + p - txx,
                m2 * u[0] - txy,
                m3 * u[0] - txz,
                total * u[0] - (u[0] * txx + u[1] * txy + u[2] * txz + conductivity * gx[3]),
            ]
            flux_y = [
                m2,
                m1 * u[1] - txy,
                m2 * u[1] + p - tyy,
                m3 * u[1] - tyz,
                total * u[1] - (u[0] * txy + u[1] * tyy + u[2] * tyz + conductivity * gy[3]),
            ]
            for f in range(5):
                FX[f, w] = flux_x[f]
                FY[f, w] = flux_y[f]
            packs_x.append(flux_x)
            packs_y.append(flux_y)
            vertical(z, (txz, tyz, tzz, conductivity * gz[3]), (m1, m2, m3, energy), u, p)
        r = r + 1
        for f in range(5):
            for k in range(HALF):
                XS[0, r, c, f, k] = pack_high(packs_x[k][f], packs_x[k + HALF][f])
                XS[1, r, c, f, k] = pack_low(packs_x[k][f], packs_x[k + HALF][f])
        send_y(r, c, [packs_y[k][f] for f in range(5) for k in range(CH)])
        for copy in exchange(r, c):
            copy.start()
        return carry

    def ghost_gradients():
        for copy in ghost_exchange():
            copy.wait_recv()
        halos = [[None] * 8 for _ in range(2)]
        for f in range(2):
            for k in range(4):
                halos[f][k], halos[f][k + 4] = unpack_x(XRG[0, f, k], XRG[1, f, k])
        merged = merge_y(YRG)
        for k in range(8):
            z = ghost - 4 + k if k < 4 else ghost + planes + k - 4
            u = [PR[f, z] for f in range(3)]
            GH[0, k] = d_x(u[0], halos[0][k]) + d_y(u[1], unpack_y(merged, k))
            GH[1, k] = d_x(u[2], halos[1][k])
            GH[2, k] = d_y(u[2], unpack_y(merged, 8 + k))

    def ghost_flux(k, carry):
        z = ghost - 4 + k + (planes + 4 - 4) * (k // 4)
        gz = [d_z(PR, f, z) for f in range(4)]
        dilation = (2.0 / 3.0 * viscosity) * (GH[0, k] + gz[2])
        tzz = (2.0 * viscosity) * gz[2] - dilation
        txz = viscosity * (GH[1, k] + gz[0])
        tyz = viscosity * (GH[2, k] + gz[1])
        vertical(
            z,
            (txz, tyz, tzz, conductivity * gz[3]),
            [QE[f, z] for f in range(1, 5)],
            [PR[f, z] for f in range(3)],
            PR[4, z],
        )
        return carry

    def slope_chunk(c, carry):
        for k in range(CH):
            w = c * CH + k
            for f in range(5):
                SL[f, w] = inner_x(FX[f, w]) + inner_y(FY[f, w]) + d_z(FZ, f, w + 4)
        return carry

    def update_chunk(section, c, carry):
        r = 2 * section + 1
        for copy in exchange(r, c):
            copy.wait_recv()
        edges = [[None] * CH for _ in range(5)]
        for f in range(5):
            for k in range(HALF):
                edges[f][k], edges[f][k + HALF] = edge_x(r, c, f, k)
        packed = [edge_y(merge_y(YR, r, c, i), YS[r, c, i]) for i in range(Y_FLUX)]
        values = []
        for k in range(CH):
            w = c * CH + k
            z = ghost + w
            q = []
            for f in range(5):
                slope = SL[f, w] + edges[f][k] + place_y(packed, CH * f + k)
                if section == 1:
                    slope_out[f, w] = slope
                    continue
                register = section_a[0] * REG[f, w] - time_step * slope
                register_out[f, w] = register
                state = QE[f, z] + section_b[0] * register
                QE[f, z] = state
                state_out[f, w] = state
                q.append(state)
            if section == 0:
                values.append(store_primitives(q, z))
        if section == 0:
            send_state(2, c, values)
        return carry

    loads[0].wait()
    pl.semaphore_wait(barrier, 2 + len(y_sides))
    lax.fori_loop(0, chunks, start_chunk, 0)
    loads[1].wait()
    loads[2].wait()
    ghost_start()
    for section in range(2):
        lax.fori_loop(0, chunks, gradient_chunk, 0)
        lax.fori_loop(0, chunks, functools.partial(flux_chunk, 2 * section), 0)
        if section == 0:
            ghost_gradients()
            loads[3].wait()
        lax.fori_loop(0, 8, ghost_flux, 0)
        lax.fori_loop(0, chunks, slope_chunk, 0)
        lax.fori_loop(0, chunks, functools.partial(update_chunk, section), 0)

    for copy in ghost_exchange():
        copy.wait_send()

    def finish(c, carry):
        for r in range(4):
            for copy in exchange(r, c):
                copy.wait_send()
        return carry

    lax.fori_loop(0, chunks, finish, 0)


def solution(mesh):
    nx, ny = mesh.shape["gx"], mesh.shape["gy"]

    def body(conserved, register, ghost_planes):
        _, planes, rows, columns = conserved.shape
        assert (rows, columns) == (8, 128) and planes % CH == 0
        chunks = planes // CH
        extended = planes + ghost_planes.shape[1]
        tile = (rows, columns)

        def vmem(*shape):
            return pltpu.VMEM(shape + tile, jnp.float32)

        dma = pltpu.SemaphoreType.DMA
        state, old, slope = pl.pallas_call(
            functools.partial(kernel, nx, ny, chunks),
            out_shape=[pltpu.VMEM(conserved.shape, jnp.float32)] * 3,
            in_specs=[pl.BlockSpec(memory_space=pltpu.HBM)] * 3,
            out_specs=[pl.BlockSpec(memory_space=pltpu.VMEM)] * 3,
            scratch_shapes=[
                vmem(5, extended),
                vmem(5, extended),
                vmem(5, planes),
                vmem(5, planes),
                vmem(5, planes),
                vmem(5, planes + 8),
                vmem(3, 8),
                vmem(4, planes),
                vmem(4, planes),
                vmem(4, planes),
                vmem(5, planes),
                vmem(2, 4, chunks, 5, HALF),
                vmem(2, 4, chunks, 5, HALF),
                vmem(4, chunks, Y_FLUX),
                vmem(2, 4, chunks, Y_FLUX),
                vmem(2, 2, 4),
                vmem(2, 2, 4),
                vmem(),
                vmem(2),
                dma((4,)),
                dma((2, 4, chunks)),
                dma((2, 4, chunks)),
                dma((2, 4, chunks)),
                dma((2, 4, chunks)),
                dma((4,)),
                dma((4,)),
            ],
            compiler_params=pltpu.CompilerParams(
                collective_id=0, has_side_effects=True, vmem_limit_bytes=60 * 1024 * 1024
            ),
        )(conserved, register, ghost_planes)
        carried = section_a[1] * old - time_step * slope
        return state + section_b[1] * carried, carried

    spec = P(None, None, "gx", "gy")
    return jax.shard_map(
        body, mesh=mesh, in_specs=(spec, spec, spec), out_specs=(spec, spec), check_vma=False
    )
```

```python
import functools

import jax
import jax.numpy as jnp
from jax import lax
from jax.experimental import pallas as pl
from jax.experimental.pallas import tpu as pltpu
from jax.sharding import PartitionSpec as P

MESH = pl.DeviceIdType.MESH

viscosity = 0.15
conductivity = 0.15 / (0.4 * 0.7)
time_step = 0.2
section_a = (-0.41789047, -1.19215169)
section_b = (0.37921031, 0.82295503)
stencil = (0.8, -0.2, 4.0 / 105.0, -1.0 / 280.0)
CH = 4
HALF = CH // 2
Y_STATE = (4 * CH + 15) // 16
Y_FLUX = (5 * CH + 15) // 16


def kernel(
    nx,
    ny,
    chunks,
    cons_hbm,
    reg_hbm,
    ghost_hbm,
    state_out,
    register_out,
    slope_out,
    QE,
    PR,
    REG,
    FX,
    FY,
    FZ,
    GH,
    DX,
    DY,
    DZ,
    SL,
    XS,
    XR,
    YS,
    YR,
    XSG,
    XRG,
    YSG,
    YRG,
    in_sem,
    xs_sem,
    xr_sem,
    ys_sem,
    yr_sem,
    gs_sem,
    gr_sem,
):
    ix = lax.axis_index("gx")
    iy = lax.axis_index("gy")
    right = lax.rem(ix + 1, nx)
    left = lax.rem(ix + nx - 1, nx)
    up = lax.rem(iy + 1, ny)
    down = lax.rem(iy + ny - 1, ny)
    y_sides = (0,) if ny == 2 else (0, 1)

    planes = chunks * CH
    ghost = ghost_hbm.shape[1] // 2
    loads = [
        pltpu.make_async_copy(cons_hbm, QE.at[:, pl.ds(ghost, planes)], in_sem.at[0]),
        pltpu.make_async_copy(ghost_hbm.at[:, pl.ds(0, ghost)], QE.at[:, pl.ds(0, ghost)], in_sem.at[1]),
        pltpu.make_async_copy(
            ghost_hbm.at[:, pl.ds(ghost, ghost)], QE.at[:, pl.ds(ghost + planes, ghost)], in_sem.at[2]
        ),
        pltpu.make_async_copy(reg_hbm, REG, in_sem.at[3]),
    ]
    for load in loads:
        load.start()

    barrier = pltpu.get_barrier_semaphore()
    pl.semaphore_signal(barrier, inc=1, device_id={"gx": left}, device_id_type=MESH)
    pl.semaphore_signal(barrier, inc=1, device_id={"gx": right}, device_id_type=MESH)
    for side in y_sides:
        pl.semaphore_signal(barrier, inc=1, device_id={"gy": (up, down)[side]}, device_id_type=MESH)

    sub = lax.broadcasted_iota(jnp.int32, (8, 128), 0)
    lane = lax.broadcasted_iota(jnp.int32, (8, 128), 1)
    low = sub < 4
    lane_group = lax.shift_right_logical(lane, 3)
    lane_first = lax.bitwise_and(lane, 7) < 4

    def x_send(way, r, c, fields):
        return pltpu.make_async_remote_copy(
            src_ref=XS.at[way, r, c, pl.ds(0, fields)],
            dst_ref=XR.at[way, r, c, pl.ds(0, fields)],
            send_sem=xs_sem.at[way, r, c],
            recv_sem=xr_sem.at[way, r, c],
            device_id={"gx": (right, left)[way]},
            device_id_type=MESH,
        )

    def y_send(way, r, c, count):
        return pltpu.make_async_remote_copy(
            src_ref=YS.at[r, c, pl.ds(0, count)],
            dst_ref=YR.at[way, r, c, pl.ds(0, count)],
            send_sem=ys_sem.at[way, r, c],
            recv_sem=yr_sem.at[way, r, c],
            device_id={"gy": (up, down)[way]},
            device_id_type=MESH,
        )

    def xg_send(way):
        return pltpu.make_async_remote_copy(
            src_ref=XSG.at[way],
            dst_ref=XRG.at[way],
            send_sem=gs_sem.at[way],
            recv_sem=gr_sem.at[way],
            device_id={"gx": (right, left)[way]},
            device_id_type=MESH,
        )

    def yg_send(way):
        return pltpu.make_async_remote_copy(
            src_ref=YSG,
            dst_ref=YRG.at[way],
            send_sem=gs_sem.at[2 + way],
            recv_sem=gr_sem.at[2 + way],
            device_id={"gy": (up, down)[way]},
            device_id_type=MESH,
        )

    def exchange(r, c):
        fields, count = ((4, Y_STATE), (5, Y_FLUX))[r % 2]
        return [x_send(way, r, c, fields) for way in (0, 1)] + [y_send(way, r, c, count) for way in y_sides]

    def ghost_exchange():
        return [xg_send(way) for way in (0, 1)] + [yg_send(way) for way in y_sides]

    def pack_high(first, second):
        return jnp.where(low, pltpu.roll(second, 4, 0), first)

    def pack_low(first, second):
        return jnp.where(low, first, pltpu.roll(second, 4, 0))

    def unpack_x(from_left, from_right):
        first = jnp.where(low, from_right, from_left)
        second = pltpu.roll(jnp.where(low, from_left, from_right), 4, 0)
        return first, second

    row = lax.bitwise_and(sub, 3)
    column = lax.bitwise_and(lane, 7)
    edge = jnp.logical_or(lane < 4, lane >= 124)
    low_weights = [jnp.where(row + d <= 3, -stencil[3 - d], 0.0) for d in range(4)]
    high_weights = [jnp.where(row >= d, stencil[3 - d], 0.0) for d in range(4)]

    def inner_x(field):
        a, b, c, _ = stencil
        after = pltpu.roll(field, 7, 0)
        before = pltpu.roll(field, 1, 0)
        middle = b * field
        return pltpu.roll(a * before + middle + c * after, 6, 0) - pltpu.roll(a * after + middle + c * before, 2, 0)

    def inner_y(field):
        a, b, c, d = stencil
        after = pltpu.roll(field, 127, 1)
        before = pltpu.roll(field, 1, 1)
        middle = c * field
        far = pltpu.roll(b * before + middle + d * after, 125, 1) - pltpu.roll(b * after + middle + d * before, 3, 1)
        return a * (after - before) + far

    def edge_x(r, c, f, k):
        gap_low = XR[0, r, c, f, k] - XS[0, r, c, f, k]
        gap_high = XR[1, r, c, f, k] - XS[1, r, c, f, k]
        at_low = low_weights[0] * gap_low
        at_high = high_weights[0] * gap_high
        for d in range(1, 4):
            at_low += low_weights[d] * pltpu.roll(gap_low, 8 - d, 0)
            at_high += high_weights[d] * pltpu.roll(gap_high, d, 0)
        return pltpu.roll(jnp.where(low, at_high, at_low), 4, 0), jnp.where(low, at_low, at_high)

    def edge_y(merged, own):
        gap = merged - own
        total = None
        for o, weight in enumerate(stencil, start=1):
            at_high = jnp.logical_and(column < 4, column + o >= 4)
            at_low = jnp.logical_and(column >= 4, column - o < 4)
            term = jnp.where(at_high, weight, 0.0) * pltpu.roll(gap, 128 - o, 1)
            term += jnp.where(at_low, -weight, 0.0) * pltpu.roll(gap, o, 1)
            total = term if total is None else total + term
        return total

    def place_y(packed, j):
        packed, j = packed[j // 16], j % 16
        return jnp.where(edge, pltpu.roll(packed, (128 - (8 * j + 4)) % 128, 1), 0.0)

    def pack_y(items):
        packed = None
        for j, item in enumerate(items):
            turned = pltpu.roll(item, (8 * j + 4) % 128, 1)
            packed = turned if packed is None else jnp.where(lane_group == j, turned, packed)
        return packed

    def send_y(r, c, items):
        for i in range(0, len(items), 16):
            YS[r, c, i // 16] = pack_y(items[i : i + 16])

    def merge_y(ref, *index):
        if ny == 2:
            return ref[(0,) + index]
        return jnp.where(lane_first, ref[(0,) + index], ref[(1,) + index])

    def unpack_y(merged, j):
        return pltpu.roll(merged, (128 - (8 * j + 4)) % 128, 1)

    def d_x(field, halo):
        total = None
        for s, weight in enumerate(stencil, start=1):
            plus = pltpu.roll(jnp.where(sub < s, halo, field), 8 - s, 0)
            minus = pltpu.roll(jnp.where(sub >= 8 - s, halo, field), s, 0)
            term = weight * (plus - minus)
            total = term if total is None else total + term
        return total

    def d_y(field, halo):
        total = None
        for s, weight in enumerate(stencil, start=1):
            plus = pltpu.roll(jnp.where(lane < s, halo, field), 128 - s, 1)
            minus = pltpu.roll(jnp.where(lane >= 128 - s, halo, field), s, 1)
            term = weight * (plus - minus)
            total = term if total is None else total + term
        return total

    def d_z(ref, f, z):
        total = None
        for s, weight in enumerate(stencil, start=1):
            term = weight * (ref[f, z + s] - ref[f, z - s])
            total = term if total is None else total + term
        return total

    def primitives(q):
        inverse = 1.0 / q[0]
        speeds = [q[1] * inverse, q[2] * inverse, q[3] * inverse]
        kinetic = 0.5 * (q[1] * speeds[0] + q[2] * speeds[1] + q[3] * speeds[2])
        pressure = 0.4 * (q[4] - kinetic)
        return speeds + [1.4 * pressure * inverse, pressure]

    def store_primitives(q, z):
        values = primitives(q)
        for f in range(5):
            PR[f, z] = values[f]
        return values

    def send_state(r, c, values):
        for f in range(4):
            for k in range(HALF):
                XS[0, r, c, f, k] = pack_high(values[k][f], values[k + HALF][f])
                XS[1, r, c, f, k] = pack_low(values[k][f], values[k + HALF][f])
        copies = exchange(r, c)
        for copy in copies[:2]:
            copy.start()
        send_y(r, c, [values[k][f] for f in range(4) for k in range(CH)])
        for copy in copies[2:]:
            copy.start()

    def start_chunk(c, carry):
        values = []
        for k in range(CH):
            z = ghost + c * CH + k
            values.append(store_primitives([QE[f, z] for f in range(5)], z))
        send_state(0, c, values)
        return carry

    def ghost_start():
        near = []
        for z in list(range(ghost)) + list(range(ghost + planes, 2 * ghost + planes)):
            values = store_primitives([QE[f, z] for f in range(5)], z)
            if ghost - 4 <= z < ghost + planes + 4:
                near.append(values)
        for f, field in enumerate((0, 2)):
            for k in range(4):
                XSG[0, f, k] = pack_high(near[k][field], near[k + 4][field])
                XSG[1, f, k] = pack_low(near[k][field], near[k + 4][field])
        YSG[...] = pack_y([near[k][field] for field in (1, 2) for k in range(8)])
        for copy in ghost_exchange():
            copy.start()

    def vertical(z, grads, q, u, p):
        m1, m2, m3, energy = q
        txz, tyz, tzz, heat = grads
        FZ[0, z - 4] = m3
        FZ[1, z - 4] = m1 * u[2] - txz
        FZ[2, z - 4] = m2 * u[2] - tyz
        FZ[3, z - 4] = m3 * u[2] + p - tzz
        FZ[4, z - 4] = (energy + p) * u[2] - (u[0] * txz + u[1] * tyz + u[2] * tzz + heat)

    def gradient_chunk(c, carry):
        for k in range(CH):
            w = c * CH + k
            for f in range(4):
                field = PR[f, ghost + w]
                DX[f, w] = inner_x(field)
                DY[f, w] = inner_y(field)
                DZ[f, w] = d_z(PR, f, ghost + w)
        return carry

    def flux_chunk(r, c, carry):
        for copy in exchange(r, c):
            copy.wait_recv()
        edges = [[None] * CH for _ in range(4)]
        for f in range(4):
            for k in range(HALF):
                edges[f][k], edges[f][k + HALF] = edge_x(r, c, f, k)
        packed = [edge_y(merge_y(YR, r, c, i), YS[r, c, i]) for i in range(Y_STATE)]
        packs_x = []
        packs_y = []
        downs = []
        for k in range(CH):
            z = ghost + c * CH + k
            value = [PR[f, z] for f in range(4)]
            w = c * CH + k
            gx = [DX[f, w] + edges[f][k] for f in range(4)]
            gy = [DY[f, w] + place_y(packed, CH * f + k) for f in range(4)]
            gz = [DZ[f, w] for f in range(4)]
            u = value[:3]
            p = PR[4, z]
            m1, m2, m3, energy = [QE[f, z] for f in range(1, 5)]
            dilation = (2.0 / 3.0 * viscosity) * (gx[0] + gy[1] + gz[2])
            txx = (2.0 * viscosity) * gx[0] - dilation
            tyy = (2.0 * viscosity) * gy[1] - dilation
            tzz = (2.0 * viscosity) * gz[2] - dilation
            txy = viscosity * (gx[1] + gy[0])
            txz = viscosity * (gx[2] + gz[0])
            tyz = viscosity * (gy[2] + gz[1])
            total = energy + p
            flux_x = [
                m1,
                m1 * u[0] + p - txx,
                m2 * u[0] - txy,
                m3 * u[0] - txz,
                total * u[0] - (u[0] * txx + u[1] * txy + u[2] * txz + conductivity * gx[3]),
            ]
            flux_y = [
                m2,
                m1 * u[1] - txy,
                m2 * u[1] + p - tyy,
                m3 * u[1] - tyz,
                total * u[1] - (u[0] * txy + u[1] * tyy + u[2] * tyz + conductivity * gy[3]),
            ]
            packs_x.append(flux_x)
            packs_y.append(flux_y)
            downs.append((z, (txz, tyz, tzz, conductivity * gz[3]), (m1, m2, m3, energy), u, p))
        r = r + 1
        copies = exchange(r, c)
        for f in range(5):
            for k in range(HALF):
                XS[0, r, c, f, k] = pack_high(packs_x[k][f], packs_x[k + HALF][f])
                XS[1, r, c, f, k] = pack_low(packs_x[k][f], packs_x[k + HALF][f])
        for copy in copies[:2]:
            copy.start()
        send_y(r, c, [packs_y[k][f] for f in range(5) for k in range(CH)])
        for copy in copies[2:]:
            copy.start()
        for k in range(CH):
            for f in range(5):
                FX[f, c * CH + k] = packs_x[k][f]
                FY[f, c * CH + k] = packs_y[k][f]
            vertical(*downs[k])
        return carry

    def ghost_gradients():
        for copy in ghost_exchange():
            copy.wait_recv()
        halos = [[None] * 8 for _ in range(2)]
        for f in range(2):
            for k in range(4):
                halos[f][k], halos[f][k + 4] = unpack_x(XRG[0, f, k], XRG[1, f, k])
        merged = merge_y(YRG)
        for k in range(8):
            z = ghost - 4 + k if k < 4 else ghost + planes + k - 4
            u = [PR[f, z] for f in range(3)]
            GH[0, k] = d_x(u[0], halos[0][k]) + d_y(u[1], unpack_y(merged, k))
            GH[1, k] = d_x(u[2], halos[1][k])
            GH[2, k] = d_y(u[2], unpack_y(merged, 8 + k))

    def ghost_flux(k, carry):
        z = ghost - 4 + k + (planes + 4 - 4) * (k // 4)
        gz = [d_z(PR, f, z) for f in range(4)]
        dilation = (2.0 / 3.0 * viscosity) * (GH[0, k] + gz[2])
        tzz = (2.0 * viscosity) * gz[2] - dilation
        txz = viscosity * (GH[1, k] + gz[0])
        tyz = viscosity * (GH[2, k] + gz[1])
        vertical(
            z,
            (txz, tyz, tzz, conductivity * gz[3]),
            [QE[f, z] for f in range(1, 5)],
            [PR[f, z] for f in range(3)],
            PR[4, z],
        )
        return carry

    def slope_chunk(c, carry):
        for k in range(CH):
            w = c * CH + k
            for f in range(5):
                SL[f, w] = inner_x(FX[f, w]) + inner_y(FY[f, w]) + d_z(FZ, f, w + 4)
        return carry

    def update_chunk(section, c, carry):
        r = 2 * section + 1
        for copy in exchange(r, c):
            copy.wait_recv()
        edges = [[None] * CH for _ in range(5)]
        for f in range(5):
            for k in range(HALF):
                edges[f][k], edges[f][k + HALF] = edge_x(r, c, f, k)
        packed = [edge_y(merge_y(YR, r, c, i), YS[r, c, i]) for i in range(Y_FLUX)]
        values = []
        for k in range(CH):
            w = c * CH + k
            z = ghost + w
            q = []
            for f in range(5):
                slope = SL[f, w] + edges[f][k] + place_y(packed, CH * f + k)
                if section == 1:
                    slope_out[f, w] = slope
                    continue
                register = section_a[0] * REG[f, w] - time_step * slope
                register_out[f, w] = register
                state = QE[f, z] + section_b[0] * register
                QE[f, z] = state
                state_out[f, w] = state
                q.append(state)
            if section == 0:
                values.append(store_primitives(q, z))
        if section == 0:
            send_state(2, c, values)
        return carry

    loads[0].wait()
    pl.semaphore_wait(barrier, 2 + len(y_sides))
    lax.fori_loop(0, chunks, start_chunk, 0)
    loads[1].wait()
    loads[2].wait()
    ghost_start()
    for section in range(2):
        lax.fori_loop(0, chunks, gradient_chunk, 0)
        lax.fori_loop(0, chunks, functools.partial(flux_chunk, 2 * section), 0)
        if section == 0:
            ghost_gradients()
            loads[3].wait()
        lax.fori_loop(0, 8, ghost_flux, 0)
        lax.fori_loop(0, chunks, slope_chunk, 0)
        lax.fori_loop(0, chunks, functools.partial(update_chunk, section), 0)

    for copy in ghost_exchange():
        copy.wait_send()

    def finish(c, carry):
        for r in range(4):
            for copy in exchange(r, c):
                copy.wait_send()
        return carry

    lax.fori_loop(0, chunks, finish, 0)


def solution(mesh):
    nx, ny = mesh.shape["gx"], mesh.shape["gy"]

    def body(conserved, register, ghost_planes):
        _, planes, rows, columns = conserved.shape
        assert (rows, columns) == (8, 128) and planes % CH == 0
        chunks = planes // CH
        extended = planes + ghost_planes.shape[1]
        tile = (rows, columns)

        def vmem(*shape):
            return pltpu.VMEM(shape + tile, jnp.float32)

        dma = pltpu.SemaphoreType.DMA
        state, old, slope = pl.pallas_call(
            functools.partial(kernel, nx, ny, chunks),
            out_shape=[pltpu.VMEM(conserved.shape, jnp.float32)] * 3,
            in_specs=[pl.BlockSpec(memory_space=pltpu.HBM)] * 3,
            out_specs=[pl.BlockSpec(memory_space=pltpu.VMEM)] * 3,
            scratch_shapes=[
                vmem(5, extended),
                vmem(5, extended),
                vmem(5, planes),
                vmem(5, planes),
                vmem(5, planes),
                vmem(5, planes + 8),
                vmem(3, 8),
                vmem(4, planes),
                vmem(4, planes),
                vmem(4, planes),
                vmem(5, planes),
                vmem(2, 4, chunks, 5, HALF),
                vmem(2, 4, chunks, 5, HALF),
                vmem(4, chunks, Y_FLUX),
                vmem(2, 4, chunks, Y_FLUX),
                vmem(2, 2, 4),
                vmem(2, 2, 4),
                vmem(),
                vmem(2),
                dma((4,)),
                dma((2, 4, chunks)),
                dma((2, 4, chunks)),
                dma((2, 4, chunks)),
                dma((2, 4, chunks)),
                dma((4,)),
                dma((4,)),
            ],
            compiler_params=pltpu.CompilerParams(
                collective_id=0, has_side_effects=True, vmem_limit_bytes=60 * 1024 * 1024
            ),
        )(conserved, register, ghost_planes)
        carried = section_a[1] * old - time_step * slope
        return state + section_b[1] * carried, carried

    spec = P(None, None, "gx", "gy")
    return jax.shard_map(
        body, mesh=mesh, in_specs=(spec, spec, spec), out_specs=(spec, spec), check_vma=False
    )
```
